256 devices in a mesh: genome: 16 (over y_hi, z), track: 16 (over y_lo, x, core).
Axes of the slice: x: 4, y: 4 (y_hi: 2, y_lo: 2; y = y_hi * 2 + y_lo), z: 8, core: 2. Of those that a mesh axis runs over, the one named last changes fastest.
Arguments:
- counts: bfloat16 [10240, 98304], P('track', 'genome'), may hold values from 0.2 to 20
- avail: int32 [80, 192], P('track', 'genome'), may hold values from 0 to 1, as said below
- track_factors: float32 [10240, 64], P('track'), may hold values from 0.1 to 1
- bin_factors: float32 [64, 98304], P(None, 'genome'), may hold values from 0.1 to 1
Outputs:
- new_tracks: float32 [10240, 64], P('track')
- new_bins: float32 [64, 98304], P(None, 'genome')
The draws below stay inside these ranges and needn't reach their ends.
Inputs may be any that keep to these rules, and one draw needn't show every extreme that they name: Every block row and every block column of avail holds a 1.
All inputs are finite; a program needn't handle non-finite values.
Results may differ from the reference program's by a relative error of at most 0.00043.
Values sent between devices are 32-bit elements; how exact they have to be, the bound alone decides.
A program may use at most 128 MiB of HBM per device.

```python
import math
import jax
import jax.numpy as jnp
from jax import lax

K = 64
TRK_DEV = 640
BIN_DEV = 6144
ITERS = 2
TRACKS = 10240
BINS = 98304
TBLK = 80
BBLK = 192
N_GENOME = 16


def draw_avail(key, part):
    key = jax.random.fold_in(key, 5)
    first, second = jax.random.split(key)
    levels = jax.random.randint(first, (TBLK, 1), 2, 9)
    values = jax.random.randint(second, (TBLK, BBLK), 0, 8)
    rows = jnp.arange(TBLK, dtype=jnp.int32)[:, None]
    cols = jnp.arange(BBLK, dtype=jnp.int32)[None, :]
    fixed = (rows + cols) % 3 == 0
    return jnp.where((values < levels) | fixed, 1, 0).astype(jnp.int32)


def draw_counts(key, part):
    key = jax.random.fold_in(key, 11)
    first, second, third = jax.random.split(key, 3)
    weights = (0.4, 0.3, 0.3)
    coarse = jax.random.uniform(first, (TRACKS // TRK_DEV, BINS // BIN_DEV), jnp.float32)
    coarse = jnp.repeat(jnp.repeat(coarse, TRK_DEV // 128, axis=0), BIN_DEV // 512, axis=1)
    blocks = jax.random.uniform(second, (TBLK, BBLK), jnp.float32)
    noise = jax.random.uniform(third, (TBLK, 128, BBLK, 512), jnp.float32)
    level = weights[0] * coarse + weights[1] * blocks
    spread = level[:, None, :, None] + weights[2] * noise
    values = 0.2 * jnp.exp(math.log(100.0) * spread)
    return values.reshape(TRACKS, BINS).astype(jnp.bfloat16)


def draw_track_factors(key, part):
    key = jax.random.fold_in(key, 13)
    first, second, third = jax.random.split(key, 3)
    weights = (0.5, 0.2, 0.3)
    coarse = jnp.repeat(jax.random.uniform(first, (TRACKS // TRK_DEV, K), jnp.float32), TRK_DEV, axis=0)
    blocks = jnp.repeat(jax.random.uniform(second, (TBLK, K), jnp.float32), 128, axis=0)
    noise = jax.random.uniform(third, (TRACKS, K), jnp.float32)
    spread = weights[0] * coarse + weights[1] * blocks + weights[2] * noise
    return (0.1 * jnp.exp(math.log(10.0) * spread)).astype(jnp.float32)


def draw_bin_factors(key, part):
    key = jax.random.fold_in(key, 17)
    first, second, third = jax.random.split(key, 3)
    weights = (0.5, 0.2, 0.3)
    coarse = jnp.repeat(jax.random.uniform(first, (K, BINS // BIN_DEV), jnp.float32), BIN_DEV, axis=1)
    blocks = jnp.repeat(jax.random.uniform(second, (K, BBLK), jnp.float32), 512, axis=1)
    noise = jax.random.uniform(third, (K, BINS), jnp.float32)
    spread = weights[0] * coarse + weights[1] * blocks + weights[2] * noise
    return (0.1 * jnp.exp(math.log(10.0) * spread)).astype(jnp.float32)


def setup_inputs(seed: int = 0) -> dict:
    arg_keys = jax.random.split(jax.random.key(seed), 5)
    counts = draw_counts(jax.random.fold_in(arg_keys[4], 71), 0)
    avail = draw_avail(jax.random.fold_in(arg_keys[4], 71), 0)
    track_factors = draw_track_factors(jax.random.fold_in(arg_keys[4], 71), 0)
    bin_factors = draw_bin_factors(jax.random.fold_in(arg_keys[4], 71), 0)
    return dict(counts=counts, avail=avail, track_factors=track_factors, bin_factors=bin_factors)


def ratio_block(values, keep, w_low, h_low):
    recon = jnp.dot(w_low, h_low, preferred_element_type=jnp.float32)
    return jnp.where(keep, values.astype(jnp.float32) / recon, 0.0).astype(jnp.bfloat16)


def reference(counts, avail, track_factors, bin_factors):
    w_now = track_factors
    h_now = bin_factors
    avail_float = avail.astype(jnp.float32)
    row_keep = jnp.repeat(avail > 0, 128, axis=0)
    for step in range(ITERS):
        w_low = w_now.astype(jnp.bfloat16)
        w_blocks = w_now.reshape(TBLK, 128, K).sum(axis=1)
        den_block = jnp.dot(avail_float.T, w_blocks, precision=lax.Precision.HIGHEST)
        den_bins = jnp.repeat(den_block.T, 512, axis=1)

        def bin_piece(index):
            start = (index * BIN_DEV).astype(jnp.int32)
            values = lax.dynamic_slice_in_dim(counts, start, BIN_DEV, 1)
            keep = jnp.repeat(lax.dynamic_slice_in_dim(row_keep, (index * (BIN_DEV // 512)).astype(jnp.int32), BIN_DEV // 512, 1), 512, axis=1)
            h_low = lax.dynamic_slice_in_dim(h_now, start, BIN_DEV, 1).astype(jnp.bfloat16)
            ratio = ratio_block(values, keep, w_low, h_low)
            return jnp.dot(ratio.T, w_low, preferred_element_type=jnp.float32).T

        pieces = lax.map(bin_piece, jnp.arange(N_GENOME, dtype=jnp.int32))
        num_bins = jnp.transpose(pieces, (1, 0, 2)).reshape(K, BINS)
        h_now = h_now * num_bins / den_bins

        h_low_all = h_now.astype(jnp.bfloat16)
        h_blocks = h_now.reshape(K, BBLK, 512).sum(axis=2)
        den_tracks = jnp.repeat(jnp.dot(avail_float, h_blocks.T, precision=lax.Precision.HIGHEST), 128, axis=0)

        def track_piece(total, index):
            start = (index * BIN_DEV).astype(jnp.int32)
            values = lax.dynamic_slice_in_dim(counts, start, BIN_DEV, 1)
            keep = jnp.repeat(lax.dynamic_slice_in_dim(row_keep, (index * (BIN_DEV // 512)).astype(jnp.int32), BIN_DEV // 512, 1), 512, axis=1)
            h_low = lax.dynamic_slice_in_dim(h_low_all, start, BIN_DEV, 1)
            ratio = ratio_block(values, keep, w_low, h_low)
            return total + jnp.dot(ratio, h_low.T, preferred_element_type=jnp.float32), None

        num_tracks, unused = lax.scan(track_piece, jnp.zeros((TRACKS, K), jnp.float32), jnp.arange(N_GENOME, dtype=jnp.int32))
        w_now = w_now * num_tracks / den_tracks
    return w_now, h_now
```

```python
import functools

import jax
import jax.numpy as jnp
from jax import lax
from jax.experimental import pallas as pl
from jax.experimental.pallas import tpu as pltpu
from jax.sharding import PartitionSpec as P

ITERS = 2
K = 64
ROWS = 640
COLS = 6144
TB = 128
BB = 512
NT = ROWS // TB
NB = COLS // BB
NC = NB // 2
HALF = 320
WIDE = 384
LAG = 3
GROUPS = ((0, 256), (256, 256), (512, 128))
MESH = pl.DeviceIdType.MESH
F32 = jnp.float32
BF16 = jnp.bfloat16


def kernel(
    counts, avail, w_in, h_in, w_out, h_out,
    cbuf, hbuf, wth, wrow, wcol, snd, own, crecv, rrecv, dsnd, dcrecv, drecv, dtot,
    acc, dacc, gsnd, grecv,
    csem, hsem, osem, cs, cr, rs, rr, gs, gr, fs, fr, ds_s, ds_r, ws, wr, us, ur,
):
    g = lax.axis_index("genome")
    t = lax.axis_index("track")
    yh, z = g // 8, g % 8
    p, c = t // 2, t % 2
    y, x = p // 4, p % 4
    sib = (g, p * 2 + (1 - c))

    def tpeer(d):
        q = ((y + d // 4) % 2) * 4 + (x + d % 4) % 4
        return q, (g, q * 2 + c)

    def gpeer(d):
        qh, qz = (yh + d // 8) % 2, (z + d % 8) % 8
        return qh, qz, (qh * 8 + qz, t)

    bar = pltpu.get_barrier_semaphore()
    pl.semaphore_signal(bar, inc=1, device_id=sib, device_id_type=MESH)
    for d in range(1, 8):
        pl.semaphore_signal(bar, inc=1, device_id=tpeer(d)[1], device_id_type=MESH)
    for d in range(1, 16):
        pl.semaphore_signal(bar, inc=1, device_id=gpeer(d)[2], device_id_type=MESH)

    def cols(b):
        return pl.ds(pl.multiple_of(b * BB, BB), BB)

    def count_copy(b):
        return pltpu.make_async_copy(counts.at[:, cols(b)], cbuf.at[:, cols(b)], csem.at[b])

    def h_copy(b):
        return pltpu.make_async_copy(h_in.at[:, cols(b)], hbuf.at[0, b], hsem.at[b])

    def out_copy(b):
        return pltpu.make_async_copy(hbuf.at[ITERS, b], h_out.at[:, cols(b)], osem.at[b])

    def start_in(j, _):
        for b in (2 * j + 1 - c, 2 * j + c):
            h_copy(b).start()
            count_copy(b).start()
        return 0

    lax.fori_loop(0, NC, start_in, 0)

    def remote(src, dst, s, r, dev):
        return pltpu.make_async_remote_copy(
            src_ref=src, dst_ref=dst, send_sem=s, recv_sem=r, device_id=dev, device_id_type=MESH
        )

    rows_p = pl.ds(pl.multiple_of(p * 8, 8), 8)
    rows_z = pl.ds(pl.multiple_of(z * 8, 8), 8)

    def core_copy(it, j):
        return remote(snd.at[it, j], crecv.at[it, j], cs.at[it, j], cr.at[it, j], sib)

    def reduce_copy(it, j, d):
        q, dev = tpeer(d)
        rows = pl.ds(pl.multiple_of(q * 8, 8), 8)
        return remote(own.at[it, j, rows], rrecv.at[it, j, d - 1], rs.at[it, j, d - 1], rr.at[it, j, d - 1], dev)

    def gather_copy(it, j, d):
        dev = tpeer(d)[1]
        ref = hbuf.at[it + 1, 2 * j + c, rows_p]
        return remote(ref, ref, gs.at[it, j, d - 1], gr.at[it, j, d - 1], dev)

    def forward_copy(it, j, which):
        ref = hbuf.at[it + 1, 2 * j + which]
        return remote(ref, ref, fs.at[it, j], fr.at[it, j], sib)

    def den_core(it):
        return remote(dsnd.at[it], dcrecv.at[it], ds_s.at[it, 0], ds_r.at[it, 0], sib)

    def den_copy(it, d):
        q, dev = tpeer(d)
        rows = pl.ds(pl.multiple_of(q * 8, 8), 8)
        return remote(dsnd.at[it + ITERS, rows], drecv.at[it, d - 1], ds_s.at[it, d], ds_r.at[it, d], dev)

    def track_copy(it, d):
        qh, qz, dev = gpeer(d)
        rows = pl.ds(pl.multiple_of(qz * 8, 8), 8)
        return remote(gsnd.at[it, qh, rows], grecv.at[it, d - 1], ws.at[it, d - 1], wr.at[it, d - 1], dev)

    def w_copy(it, d):
        dev = gpeer(d)[2]
        ref = wth.at[it + 1, yh, rows_z]
        return remote(ref, ref, us.at[it, d - 1], ur.at[it, d - 1], dev)

    lane = lax.broadcasted_iota(jnp.int32, (8, 128), 1)
    lane64 = lax.broadcasted_iota(jnp.int32, (K, 128), 1)

    def mask_of(tb, b):
        return avail[tb, b].astype(F32)

    def ratio_of(b, lo, n, h_low):
        recon = jnp.dot(wrow[lo : lo + n, :], h_low, preferred_element_type=F32)
        return (cbuf[lo : lo + n, cols(b)].astype(F32) / recon).astype(BF16)

    def bins_block(it, b):
        h_low = hbuf[it, b].astype(BF16)
        total = None
        for lo, n in GROUPS:
            ratio = ratio_of(b, lo, n, h_low)
            parts = [
                wcol[:, s : s + TB] * mask_of(s // TB, b) for s in range(lo, lo + n, TB)
            ]
            left = jnp.concatenate(parts, axis=1).astype(BF16)
            term = jnp.dot(left, ratio, preferred_element_type=F32)
            total = term if total is None else total + term
        return total

    def tracks_block(it, b):
        h_now = hbuf[it + 1, b]
        h_low = h_now.astype(BF16)
        h_sum = jnp.sum(h_now, axis=1, keepdims=True)
        keep = jnp.zeros((8, 128), F32)
        for tb in range(NT):
            keep = jnp.where(lane == 64 + tb, mask_of(tb, b), keep)
        dacc[...] += h_sum * keep[0:1, :]
        for lo, n in GROUPS:
            ratio = ratio_of(b, lo, n, h_low)
            term = lax.dot_general(h_low, ratio, (((1,), (1,)), ((), ())), preferred_element_type=F32)
            for s in range(lo, lo + n, TB):
                acc[:, s : s + TB] += term[:, s - lo : s - lo + TB] * mask_of(s // TB, b)

    def spread_w(wt):
        wcol[...] = wt.astype(BF16).astype(F32)

    w0 = w_in[...]
    wt0 = w0.T
    wrow[...] = w0.astype(BF16)
    spread_w(wt0)
    zero64 = jnp.zeros((K, 64), F32)
    wth[0, 0] = jnp.concatenate([wt0[:, :HALF], zero64], axis=1)
    wth[0, 1] = pltpu.roll(wt0[:, 256:640], HALF, 1)

    def w_full(it):
        left = wth[it, 0]
        right = pltpu.roll(wth[it, 1], 64, 1)
        mid = jnp.where(lane64 < 64, left[:, 256:384], right[:, 0:128])
        return jnp.concatenate([left[:, 0:256], mid, right[:, 128:384]], axis=1)

    def iteration(it, _):
        wt = w_full(it)
        den = jnp.zeros((K, 128), F32)
        for tb in range(NT):
            row = jnp.zeros((8, 128), F32)
            for b in range(NB):
                row = jnp.where(lane == b, mask_of(tb, b), row)
            w_sum = jnp.sum(wt[:, tb * TB : (tb + 1) * TB], axis=1, keepdims=True)
            den = den + w_sum * row[0:1, :]
        dsnd[it] = den

        @pl.when(it == 0)
        def _():
            pl.semaphore_wait(bar, 23)

        den_core(it).start()

        def stage_b(j):
            @pl.when(j == 0)
            def _():
                den_core(it).wait_recv()
                dsnd[it + ITERS] = dsnd[it] + dcrecv[it]
                for d in range(1, 8):
                    den_copy(it, d).start()

            core_copy(it, j).wait_recv()
            own[it, j] = own[it, j] + crecv[it, j]
            for d in range(1, 8):
                reduce_copy(it, j, d).start()

        def first(j, _):
            @pl.when(it == 0)
            def _():
                for b in (2 * j + 1 - c, 2 * j + c):
                    h_copy(b).wait()
                    count_copy(b).wait()

            snd[it, j] = bins_block(it, 2 * j + 1 - c)
            core_copy(it, j).start()

            @pl.when(j > 0)
            def _():
                stage_b(j - 1)

            own[it, j] = bins_block(it, 2 * j + c)
            return 0

        lax.fori_loop(0, NC, first, 0)
        stage_b(NC - 1)

        acc[...] = jnp.zeros((K, ROWS), F32)
        dacc[...] = jnp.zeros((K, 128), F32)

        def stage_c(j):
            @pl.when(j == 0)
            def _():
                tot = dsnd[it + ITERS, rows_p]
                for d in range(1, 8):
                    den_copy(it, d).wait_recv()
                    tot = tot + drecv[it, d - 1]
                dtot[...] = tot

            tot = own[it, j, rows_p]
            for d in range(1, 8):
                reduce_copy(it, j, d).wait_recv()
                tot = tot + rrecv[it, j, d - 1]
            b = 2 * j + c
            den = jnp.sum(jnp.where(lane == b, dtot[...], 0.0), axis=1, keepdims=True)
            hbuf[it + 1, b, rows_p] = hbuf[it, b, rows_p] * tot / den
            for d in range(1, 8):
                gather_copy(it, j, d).start()

        def stage_d(j):
            for d in range(1, 8):
                gather_copy(it, j, d).wait_recv()
            forward_copy(it, j, c).start()

        def stage_e(j):
            tracks_block(it, 2 * j + c)
            forward_copy(it, j, 1 - c).wait_recv()
            tracks_block(it, 2 * j + 1 - c)

            @pl.when(it == ITERS - 1)
            def _():
                out_copy(2 * j + c).start()
                out_copy(2 * j + 1 - c).start()

        def second(k, _):
            @pl.when(k < NC)
            def _():
                stage_c(k)

            @pl.when((k >= LAG) & (k < NC + LAG))
            def _():
                stage_d(k - LAG)

            @pl.when(k >= LAG + 1)
            def _():
                stage_e(k - LAG - 1)

            return 0

        lax.fori_loop(0, NC + LAG + 1, second, 0)

        full = acc[...]
        dvec = dacc[...]
        gsnd[it, 0, :, 0:256] = full[:, 0:256]
        gsnd[it, 0, :, 256:384] = jnp.where(lane64 < 64, full[:, 256:384], dvec)
        right = pltpu.roll(full[:, 256:640], HALF, 1)
        gsnd[it, 1, :, 0:256] = right[:, 0:256]
        gsnd[it, 1, :, 256:384] = jnp.where(lane64 < 64, right[:, 256:384], dvec)
        for d in range(1, 16):
            track_copy(it, d).start()
        tot = gsnd[it, yh, rows_z]
        for d in range(1, 16):
            track_copy(it, d).wait_recv()
            tot = tot + grecv[it, d - 1]
        wide = lax.broadcasted_iota(jnp.int32, (8, WIDE), 1)
        block = (wide + yh * HALF) // TB
        den = jnp.ones((8, WIDE), F32)
        for tb in range(NT):
            den = jnp.where(block == tb, tot[:, HALF + tb : HALF + tb + 1], den)
        wth[it + 1, yh, rows_z] = wth[it, yh, rows_z] * tot / den
        for d in range(1, 16):
            w_copy(it, d).start()
        for d in range(1, 16):
            w_copy(it, d).wait_recv()
        wt = w_full(it + 1)
        spread_w(wt)
        w_new = wt.T
        wrow[...] = w_new.astype(BF16)
        w_out[...] = w_new

        den_core(it).wait_send()
        for d in range(1, 8):
            den_copy(it, d).wait_send()
        for d in range(1, 16):
            track_copy(it, d).wait_send()
            w_copy(it, d).wait_send()

        def drain(j, _):
            core_copy(it, j).wait_send()
            forward_copy(it, j, c).wait_send()
            for d in range(1, 8):
                reduce_copy(it, j, d).wait_send()
                gather_copy(it, j, d).wait_send()
            return 0

        lax.fori_loop(0, NC, drain, 0)
        return 0

    lax.fori_loop(0, ITERS, iteration, 0)

    def finish(b, _):
        out_copy(b).wait()
        return 0

    lax.fori_loop(0, NB, finish, 0)


def body(counts, avail, track_factors, bin_factors):
    dma = pltpu.SemaphoreType.DMA
    vmem = pltpu.VMEM
    return pl.pallas_call(
        kernel,
        name="factorize",
        out_shape=(
            jax.ShapeDtypeStruct((ROWS, K), F32),
            jax.ShapeDtypeStruct((K, COLS), F32),
        ),
        in_specs=[
            pl.BlockSpec(memory_space=pl.ANY),
            pl.BlockSpec(memory_space=pltpu.SMEM),
            pl.BlockSpec(memory_space=pltpu.VMEM),
            pl.BlockSpec(memory_space=pl.ANY),
        ],
        out_specs=(
            pl.BlockSpec(memory_space=pltpu.VMEM),
            pl.BlockSpec(memory_space=pl.ANY),
        ),
        scratch_shapes=[
            vmem((ROWS, COLS), BF16),
            vmem((ITERS + 1, NB, K, BB), F32),
            vmem((ITERS + 1, 2, K, WIDE), F32),
            vmem((ROWS, K), BF16),
            vmem((K, ROWS), F32),
            vmem((ITERS, NC, K, BB), F32),
            vmem((ITERS, NC, K, BB), F32),
            vmem((ITERS, NC, K, BB), F32),
            vmem((ITERS, NC, 7, 8, BB), F32),
            vmem((2 * ITERS, K, 128), F32),
            vmem((ITERS, K, 128), F32),
            vmem((ITERS, 7, 8, 128), F32),
            vmem((8, 128), F32),
            vmem((K, ROWS), F32),
            vmem((K, 128), F32),
            vmem((ITERS, 2, K, WIDE), F32),
            vmem((ITERS, 15, 8, WIDE), F32),
            dma((NB,)), dma((NB,)), dma((NB,)),
            dma((ITERS, NC)), dma((ITERS, NC)),
            dma((ITERS, NC, 7)), dma((ITERS, NC, 7)),
            dma((ITERS, NC, 7)), dma((ITERS, NC, 7)),
            dma((ITERS, NC)), dma((ITERS, NC)),
            dma((ITERS, 8)), dma((ITERS, 8)),
            dma((ITERS, 15)), dma((ITERS, 15)),
            dma((ITERS, 15)), dma((ITERS, 15)),
        ],
        compiler_params=pltpu.CompilerParams(
            collective_id=0, has_side_effects=True, vmem_limit_bytes=56 * 1024 * 1024
        ),
    )(counts, avail, track_factors, bin_factors)


def solution(mesh):
    placed = (P("track", "genome"), P("track", "genome"), P("track", None), P(None, "genome"))
    return jax.shard_map(
        body,
        mesh=mesh,
        in_specs=placed,
        out_specs=(P("track", None), P(None, "genome")),
        check_vma=False,
    )
```

```python
import jax
import jax.numpy as jnp
from jax import lax
from jax.experimental import pallas as pl
from jax.experimental.pallas import tpu as pltpu
from jax.sharding import PartitionSpec as P

ITERS = 2
K = 64
ROWS = 640
COLS = 6144
TB = 128
BB = 512
NT = ROWS // TB
NB = COLS // BB
NC = NB // 2
HALF = 320
WIDE = 384
LAG = 6
FAR = (12, 11, 13, 4, 10, 14, 3, 5, 9, 15, 2, 6, 8, 1, 7)
NEAR = (6, 2, 5, 1, 7, 3, 4)
TILES = (2, 0, 1)
CB = 2 * BB
MESH = pl.DeviceIdType.MESH
F32 = jnp.float32
BF16 = jnp.bfloat16


def kernel(
    counts, avail_in, w_in, h_in, w_out, h_out,
    avail, wbuf, cbuf, hbuf, wth, wrow, wcol, part, crecv, rrecv, dsnd, dcrecv, drecv, dtot,
    acc, dacc, gsnd, grecv,
    csem, hsem, osem, wsem, send, cr, rr, gr, fr, dr, wr,
):
    g = lax.axis_index("genome")
    t = lax.axis_index("track")
    yh, z = g // 8, g % 8
    p, c = t // 2, t % 2
    y, x = p // 4, p % 4
    sib = (g, p * 2 + (1 - c))

    def tpeer(d):
        q = ((y + d // 4) % 2) * 4 + (x + d % 4) % 4
        return q, (g, q * 2 + c)

    def gpeer(d):
        qh, qz = (yh + d // 8) % 2, (z + d % 8) % 8
        return qh, qz, (qh * 8 + qz, t)

    def cols(j):
        return pl.ds(pl.multiple_of(j * CB, CB), CB)

    def half(which):
        return pl.ds(pl.multiple_of(which * BB, BB), BB)

    def count_copy(j):
        return pltpu.make_async_copy(counts.at[:, cols(j)], cbuf.at[:, cols(j)], csem.at[j])

    def h_copy(j):
        return pltpu.make_async_copy(h_in.at[:, cols(j)], hbuf.at[0, j], hsem.at[j])

    def out_copy(j):
        return pltpu.make_async_copy(hbuf.at[ITERS, j], h_out.at[:, cols(j)], osem.at[j])

    def start_in(j, _):
        h_copy(j).start()
        count_copy(j).start()
        return 0

    w_copy_in = pltpu.make_async_copy(w_in, wbuf, wsem.at[0])
    w_copy_out = pltpu.make_async_copy(wbuf, w_out, wsem.at[1])
    w_copy_in.start()
    avail_copy = pltpu.make_async_copy(avail_in, avail, wsem.at[2])
    avail_copy.start()
    start_in(0, 0)

    bar = pltpu.get_barrier_semaphore()
    for d in FAR:
        pl.semaphore_signal(bar, inc=1, device_id=gpeer(d)[2], device_id_type=MESH)
    for d in range(1, 8):
        pl.semaphore_signal(bar, inc=1, device_id=tpeer(d)[1], device_id_type=MESH)
    pl.semaphore_signal(bar, inc=1, device_id=sib, device_id_type=MESH)

    def remote(src, dst, s, r, dev):
        return pltpu.make_async_remote_copy(
            src_ref=src, dst_ref=dst, send_sem=s, recv_sem=r, device_id=dev, device_id_type=MESH
        )

    rows_p = pl.ds(pl.multiple_of(p * 8, 8), 8)
    rows_z = pl.ds(pl.multiple_of(z * 8, 8), 8)

    def core_copy(it, j):
        return remote(part.at[it, j, :, half(1 - c)], crecv.at[it, j], send.at[0], cr.at[it, j], sib)

    def reduce_copy(it, j, d):
        q, dev = tpeer(d)
        rows = pl.ds(pl.multiple_of(q * 8, 8), 8)
        return remote(part.at[it, j, rows, half(c)], rrecv.at[it, j, d - 1], send.at[1], rr.at[it, j], dev)

    def reduce_all(it, j):
        return remote(rrecv.at[it, j], rrecv.at[it, j], send.at[1], rr.at[it, j], sib)

    def gather_copy(it, j, d):
        ref = hbuf.at[it + 1, j, rows_p, half(c)]
        return remote(ref, ref, send.at[2], gr.at[it, j], tpeer(d)[1])

    def gather_all(it, j):
        return remote(rrecv.at[it, j], rrecv.at[it, j], send.at[2], gr.at[it, j], sib)

    def forward_copy(it, j, which):
        ref = hbuf.at[it + 1, j, :, half(which)]
        return remote(ref, ref, send.at[3], fr.at[it, j], sib)

    def den_core(it):
        return remote(dsnd.at[it], dcrecv.at[it], send.at[4], dr.at[it, 0], sib)

    def den_copy(it, d):
        q, dev = tpeer(d)
        rows = pl.ds(pl.multiple_of(q * 8, 8), 8)
        return remote(dsnd.at[it + ITERS, rows], drecv.at[it, d - 1], send.at[5], dr.at[it, 1], dev)

    def den_all(it):
        return remote(drecv.at[it], drecv.at[it], send.at[5], dr.at[it, 1], sib)

    def tile(k):
        return slice(k * 128, (k + 1) * 128)

    def track_copy(it, k, d):
        qh, qz, dev = gpeer(d)
        rows = pl.ds(pl.multiple_of(qz * 8, 8), 8)
        return remote(
            gsnd.at[it, qh, rows, tile(k)], grecv.at[it, k, d - 1], send.at[6], wr.at[it, k], dev
        )

    def w_copy(it, k, d):
        ref = wth.at[it + 1, yh, rows_z, tile(k)]
        return remote(ref, ref, send.at[7], wr.at[it, 3], gpeer(d)[2])

    lane = lax.broadcasted_iota(jnp.int32, (8, 128), 1)
    lane64 = lax.broadcasted_iota(jnp.int32, (K, 128), 1)

    def mask_of(tb, b):
        return avail[tb, b].astype(F32)

    def ratio_of(b, h_low):
        recon = jnp.dot(wrow[...], h_low, preferred_element_type=F32)
        return (cbuf[:, half(b)].astype(F32) / recon).astype(BF16)

    def bins_half(it, j, which):
        b = 2 * j + which
        ratio = ratio_of(b, hbuf[it, j, :, half(which)].astype(BF16))
        left = jnp.concatenate(
            [wcol[:, tb * TB : (tb + 1) * TB] * mask_of(tb, b) for tb in range(NT)], axis=1
        ).astype(BF16)
        part[it, j, :, half(which)] = jnp.dot(left, ratio, preferred_element_type=F32)

    def tracks_half(it, j, which):
        b = 2 * j + which
        h_now = hbuf[it + 1, j, :, half(which)]
        h_low = h_now.astype(BF16)
        ratio = ratio_of(b, h_low)
        h_sum = jnp.sum(h_now, axis=1, keepdims=True)
        keep = jnp.zeros((8, 128), F32)
        for tb in range(NT):
            keep = jnp.where(lane == 64 + tb, mask_of(tb, b), keep)
        dacc[...] += h_sum * keep[0:1, :]
        term = lax.dot_general(h_low, ratio, (((1,), (1,)), ((), ())), preferred_element_type=F32)
        for tb in range(NT):
            s = slice(tb * TB, (tb + 1) * TB)
            acc[:, s] += term[:, s] * mask_of(tb, b)

    def spread_w(wt):
        wcol[...] = wt.astype(BF16).astype(F32)
        wrow[...] = wt.T.astype(BF16)

    w_copy_in.wait()
    avail_copy.wait()
    wt0 = wbuf[...]
    spread_w(wt0)
    wth[0, 0] = jnp.concatenate([wt0[:, :HALF], jnp.zeros((K, 64), F32)], axis=1)
    wth[0, 1] = pltpu.roll(wt0[:, 256:640], HALF, 1)

    def w_full(it):
        left = wth[it, 0]
        right = pltpu.roll(wth[it, 1], 64, 1)
        mid = jnp.where(lane64 < 64, left[:, 256:384], right[:, 0:128])
        return jnp.concatenate([left[:, 0:256], mid, right[:, 128:384]], axis=1)

    def start_den(it):
        wt = w_full(it)
        den = jnp.zeros((K, 128), F32)
        for tb in range(NT):
            row = jnp.zeros((8, 128), F32)
            for b in range(NB):
                row = jnp.where(lane == b, mask_of(tb, b), row)
            w_sum = jnp.sum(wt[:, tb * TB : (tb + 1) * TB], axis=1, keepdims=True)
            den = den + w_sum * row[0:1, :]
        dsnd[it] = den
        den_core(it).start()

    def stage_b(it, j):
        core_copy(it, j).wait_recv()
        part[it, j, :, half(c)] = part[it, j, :, half(c)] + crecv[it, j]
        for d in NEAR:
            reduce_copy(it, j, d).start()

        @pl.when(j == 0)
        def _():
            den_core(it).wait_recv()
            dsnd[it + ITERS] = dsnd[it] + dcrecv[it]
            for d in range(1, 8):
                den_copy(it, d).start()

    def stage_c(it, j):
        @pl.when(j == 0)
        def _():
            den_all(it).wait_recv()
            tot = dsnd[it + ITERS, rows_p]
            for d in range(1, 8):
                tot = tot + drecv[it, d - 1]
            dtot[...] = tot

        reduce_all(it, j).wait_recv()
        tot = part[it, j, rows_p, half(c)]
        for d in range(1, 8):
            tot = tot + rrecv[it, j, d - 1]
        den = jnp.sum(jnp.where(lane == 2 * j + c, dtot[...], 0.0), axis=1, keepdims=True)
        hbuf[it + 1, j, rows_p, half(c)] = hbuf[it, j, rows_p, half(c)] * tot / den
        for d in NEAR:
            gather_copy(it, j, d).start()

    def stage_d(it, j):
        gather_all(it, j).wait_recv()
        forward_copy(it, j, c).start()
        tracks_half(it, j, c)

    def stage_e(it, j):
        forward_copy(it, j, 1 - c).wait_recv()
        tracks_half(it, j, 1 - c)

        @pl.when(it == ITERS - 1)
        def _():
            out_copy(j).start()

    def pack_tracks(it):
        full = acc[...]
        dvec = dacc[...]
        gsnd[it, 0, :, 0:256] = full[:, 0:256]
        gsnd[it, 0, :, 256:384] = jnp.where(lane64 < 64, full[:, 256:384], dvec)
        right = pltpu.roll(full[:, 256:640], HALF, 1)
        gsnd[it, 1, :, 0:256] = right[:, 0:256]
        gsnd[it, 1, :, 256:384] = jnp.where(lane64 < 64, right[:, 256:384], dvec)

    def send_tracks(it):
        for k in TILES:
            for d in FAR:
                track_copy(it, k, d).start()

    def wait_tracks(it, k):
        remote(grecv.at[it, k], grecv.at[it, k], send.at[6], wr.at[it, k], sib).wait_recv()

    def update_w(it):
        divisor = None
        for k in TILES:
            wait_tracks(it, k)
            tot = gsnd[it, yh, rows_z, tile(k)]
            for d in range(1, 16):
                tot = tot + grecv[it, k, d - 1]
            if divisor is None:
                divisor = [tot[:, 64 + tb : 65 + tb] for tb in range(NT)]
            block = (lane + (yh * HALF + k * 128)) // TB
            den = jnp.ones((8, 128), F32)
            for tb in range(NT):
                den = jnp.where(block == tb, divisor[tb], den)
            wth[it + 1, yh, rows_z, tile(k)] = wth[it, yh, rows_z, tile(k)] * tot / den
            for d in FAR:
                w_copy(it, k, d).start()

    def wait_w(it):
        remote(grecv.at[it], grecv.at[it], send.at[7], wr.at[it, 3], sib).wait_recv()

    def iteration(it, _):
        acc[...] = jnp.zeros((K, ROWS), F32)
        dacc[...] = jnp.zeros((K, 128), F32)

        def first(j, _):
            @pl.when(it == 0)
            def _():
                h_copy(j).wait()
                count_copy(j).wait()

            @pl.when((it == 0) & (j == 0))
            def _():
                lax.fori_loop(1, NC, start_in, 0)

            bins_half(it, j, 1 - c)

            @pl.when((it == 0) & (j == 0))
            def _():
                pl.semaphore_wait(bar, 23)

            core_copy(it, j).start()

            @pl.when(j == 0)
            def _():
                start_den(it)

            @pl.when(j > 0)
            def _():
                stage_b(it, j - 1)

            bins_half(it, j, c)
            return 0

        lax.fori_loop(0, NC, first, 0)
        stage_b(it, NC - 1)

        def second(k, _):
            @pl.when(k < NC)
            def _():
                stage_c(it, k)

            @pl.when((k >= LAG) & (k < NC + LAG))
            def _():
                stage_d(it, k - LAG)

            @pl.when(k > LAG)
            def _():
                stage_e(it, k - LAG - 1)

            return 0

        lax.fori_loop(0, NC + LAG + 1, second, 0)
        pack_tracks(it)
        send_tracks(it)
        update_w(it)
        wait_w(it)
        wt = w_full(it + 1)

        @pl.when(it < ITERS - 1)
        def _():
            spread_w(wt)

        wbuf[...] = wt
        return 0

    lax.fori_loop(0, ITERS, iteration, 0)
    w_copy_out.start()

    def finish(j, _):
        out_copy(j).wait()
        return 0

    lax.fori_loop(0, NC, finish, 0)

    def sent(ref, s):
        remote(ref, ref, send.at[s], dr.at[0, 0], sib).wait_send()

    sent(crecv, 0)
    sent(rrecv, 1)
    sent(rrecv, 2)
    sent(crecv, 3)
    sent(dcrecv, 4)
    sent(drecv, 5)
    sent(grecv, 6)
    sent(grecv, 7)
    w_copy_out.wait()


def settle(w_ref, h_ref, w_out, h_out, sem):
    copies = [pltpu.make_async_copy(w_ref, w_out, sem.at[NC])]
    for j in range(NC):
        span = slice(j * CB, (j + 1) * CB)
        copies.append(pltpu.make_async_copy(h_ref.at[:, span], h_out.at[:, span], sem.at[j]))
    for copy in copies:
        copy.start()
    for copy in copies:
        copy.wait()


def body(counts, avail, track_factors, bin_factors):
    dma = pltpu.SemaphoreType.DMA
    vmem = pltpu.VMEM
    w_new, h_new = pl.pallas_call(
        kernel,
        name="factorize",
        out_shape=(
            pltpu.VMEM((K, ROWS), F32),
            pltpu.VMEM((K, COLS), F32),
        ),
        in_specs=[
            pl.BlockSpec(memory_space=pl.ANY),
            pl.BlockSpec(memory_space=pl.ANY),
            pl.BlockSpec(memory_space=pl.ANY),
            pl.BlockSpec(memory_space=pl.ANY),
        ],
        out_specs=(
            pl.BlockSpec(memory_space=pltpu.VMEM),
            pl.BlockSpec(memory_space=pltpu.VMEM),
        ),
        scratch_shapes=[
            pltpu.SMEM((NT, NB), jnp.int32),
            vmem((K, ROWS), F32),
            vmem((ROWS, COLS), BF16),
            vmem((ITERS + 1, NC, K, CB), F32),
            vmem((ITERS + 1, 2, K, WIDE), F32),
            vmem((ROWS, K), BF16),
            vmem((K, ROWS), F32),
            vmem((ITERS, NC, K, CB), F32),
            vmem((ITERS, NC, K, BB), F32),
            vmem((ITERS, NC, 7, 8, BB), F32),
            vmem((2 * ITERS, K, 128), F32),
            vmem((ITERS, K, 128), F32),
            vmem((ITERS, 7, 8, 128), F32),
            vmem((8, 128), F32),
            vmem((K, ROWS), F32),
            vmem((K, 128), F32),
            vmem((ITERS, 2, K, WIDE), F32),
            vmem((ITERS, 3, 15, 8, 128), F32),
            dma((NC,)),
            dma((NC,)),
            dma((NC,)),
            dma((3,)),
            dma((8,)),
            dma((ITERS, NC)),
            dma((ITERS, NC)),
            dma((ITERS, NC)),
            dma((ITERS, NC)),
            dma((ITERS, 2)),
            dma((ITERS, 4)),
        ],
        compiler_params=pltpu.CompilerParams(
            collective_id=0, has_side_effects=True, vmem_limit_bytes=56 * 1024 * 1024
        ),
    )(counts, avail, track_factors.T, bin_factors)
    anywhere = pl.BlockSpec(memory_space=pl.ANY)
    w_new, h_new = pl.pallas_call(
        settle,
        name="settle",
        out_shape=(jax.ShapeDtypeStruct((K, ROWS), F32), jax.ShapeDtypeStruct((K, COLS), F32)),
        in_specs=[anywhere, anywhere],
        out_specs=(anywhere, anywhere),
        scratch_shapes=[dma((NC + 1,))],
    )(*(pltpu.with_memory_space_constraint(v, pltpu.VMEM) for v in (w_new, h_new)))
    return w_new.T, h_new


def solution(mesh):
    placed = (P("track", "genome"), P("track", "genome"), P("track", None), P(None, "genome"))
    return jax.shard_map(
        body,
        mesh=mesh,
        in_specs=placed,
        out_specs=(P("track", None), P(None, "genome")),
        check_vma=False,
    )
```

```python
import jax
import jax.numpy as jnp
from jax import lax
from jax.experimental import pallas as pl
from jax.experimental.pallas import tpu as pltpu
from jax.sharding import PartitionSpec as P

ITERS = 2
K = 64
ROWS = 640
COLS = 6144
TB = 128
BB = 512
NT = ROWS // TB
NB = COLS // BB
NC = NB // 2
HALF = 320
WIDE = 384
LAG = 6
FAR = (12, 11, 13, 4, 10, 14, 3, 5, 9, 15, 2, 6, 8, 1, 7)
NEAR = (6, 2, 5, 1, 7, 3, 4)
PIECES = 1
SPANS = ((256, 128), (0, 256))
CB = 2 * BB
MESH = pl.DeviceIdType.MESH
F32 = jnp.float32
BF16 = jnp.bfloat16


def kernel(
    counts, avail_in, w_in, h_in, w_out, h_out,
    avail, wbuf, cbuf, hbuf, wth, wrow, wcol, part, crecv, rrecv, dsnd, dcrecv, drecv, dtot,
    acc, dacc, gsnd, grecv,
    csem, hsem, osem, wsem, send, cr, rr, gr, fr, dr, wr,
):
    g = lax.axis_index("genome")
    t = lax.axis_index("track")
    yh, z = g // 8, g % 8
    p, c = t // 2, t % 2
    y, x = p // 4, p % 4
    sib = (g, p * 2 + (1 - c))

    def tpeer(d):
        q = ((y + d // 4) % 2) * 4 + (x + d % 4) % 4
        return q, (g, q * 2 + c)

    def gpeer(d):
        qh, qz = (yh + d // 8) % 2, (z + d % 8) % 8
        return qh, qz, (qh * 8 + qz, t)

    def cols(j):
        return pl.ds(pl.multiple_of(j * CB, CB), CB)

    def half(which):
        return pl.ds(pl.multiple_of(which * BB, BB), BB)

    def count_copy(j):
        return pltpu.make_async_copy(counts.at[:, cols(j)], cbuf.at[:, cols(j)], csem.at[j])

    def h_copy(j):
        return pltpu.make_async_copy(h_in.at[:, cols(j)], hbuf.at[0, j], hsem.at[j])

    def out_copy(j):
        return pltpu.make_async_copy(hbuf.at[ITERS, j], h_out.at[:, cols(j)], osem.at[j])

    def start_in(j, _):
        h_copy(j).start()
        count_copy(j).start()
        return 0

    def first_in(which):
        rows = ROWS // PIECES
        return [
            pltpu.make_async_copy(
                counts.at[r * rows : (r + 1) * rows, half(which)],
                cbuf.at[r * rows : (r + 1) * rows, half(which)],
                csem.at[which * NC],
            )
            for r in range(PIECES)
        ]

    w_copy_in = pltpu.make_async_copy(w_in, wbuf, wsem.at[0])
    w_copy_in.start()
    avail_copy = pltpu.make_async_copy(avail_in, avail, wsem.at[1])
    avail_copy.start()
    h_copy(0).start()
    for copy in first_in(1 - c) + first_in(c):
        copy.start()

    bar = pltpu.get_barrier_semaphore()
    for d in FAR:
        pl.semaphore_signal(bar, inc=1, device_id=gpeer(d)[2], device_id_type=MESH)
    for d in range(1, 8):
        pl.semaphore_signal(bar, inc=1, device_id=tpeer(d)[1], device_id_type=MESH)
    pl.semaphore_signal(bar, inc=1, device_id=sib, device_id_type=MESH)

    def remote(src, dst, s, r, dev):
        return pltpu.make_async_remote_copy(
            src_ref=src, dst_ref=dst, send_sem=s, recv_sem=r, device_id=dev, device_id_type=MESH
        )

    rows_p = pl.ds(pl.multiple_of(p * 8, 8), 8)
    rows_z = pl.ds(pl.multiple_of(z * 8, 8), 8)

    def core_copy(it, j):
        return remote(part.at[it, j, :, half(1 - c)], crecv.at[it, j], send.at[0], cr.at[it, j], sib)

    def reduce_copy(it, j, d):
        q, dev = tpeer(d)
        rows = pl.ds(pl.multiple_of(q * 8, 8), 8)
        return remote(part.at[it, j, rows, half(c)], rrecv.at[it, j, d - 1], send.at[1], rr.at[it, j], dev)

    def reduce_all(it, j):
        return remote(rrecv.at[it, j], rrecv.at[it, j], send.at[1], rr.at[it, j], sib)

    def gather_copy(it, j, d):
        ref = hbuf.at[it + 1, j, rows_p, half(c)]
        return remote(ref, ref, send.at[2], gr.at[it, j], tpeer(d)[1])

    def gather_all(it, j):
        return remote(rrecv.at[it, j], rrecv.at[it, j], send.at[2], gr.at[it, j], sib)

    def forward_copy(it, j, which):
        ref = hbuf.at[it + 1, j, :, half(which)]
        return remote(ref, ref, send.at[3], fr.at[it, j], sib)

    def den_core(it):
        return remote(dsnd.at[it], dcrecv.at[it], send.at[4], dr.at[it, 0], sib)

    def den_copy(it, d):
        q, dev = tpeer(d)
        rows = pl.ds(pl.multiple_of(q * 8, 8), 8)
        return remote(dsnd.at[it + ITERS, rows], drecv.at[it, d - 1], send.at[5], dr.at[it, 1], dev)

    def den_all(it):
        return remote(drecv.at[it], drecv.at[it], send.at[5], dr.at[it, 1], sib)

    def track_copy(it, k, d):
        qh, qz, dev = gpeer(d)
        rows = pl.ds(pl.multiple_of(qz * 8, 8), 8)
        lo, n = SPANS[k]
        return remote(
            gsnd.at[it, qh, rows, lo : lo + n], grecv.at[it, d - 1, :, lo : lo + n], send.at[6], wr.at[it, k], dev
        )

    def w_copy(it, k, d):
        lo, n = SPANS[k]
        ref = wth.at[it + 1, yh, rows_z, lo : lo + n]
        return remote(ref, ref, send.at[7], wr.at[it, 3], gpeer(d)[2])

    lane = lax.broadcasted_iota(jnp.int32, (8, 128), 1)
    lane64 = lax.broadcasted_iota(jnp.int32, (K, 128), 1)

    def mask_of(tb, b):
        return avail[tb, b].astype(F32)

    def ratio_of(b, h_low):
        recon = jnp.dot(wrow[...], h_low, preferred_element_type=F32)
        return (cbuf[:, half(b)].astype(F32) / recon).astype(BF16)

    def bins_half(it, j, which):
        b = 2 * j + which
        ratio = ratio_of(b, hbuf[it, j, :, half(which)].astype(BF16))
        left = jnp.concatenate(
            [wcol[:, tb * TB : (tb + 1) * TB] * mask_of(tb, b) for tb in range(NT)], axis=1
        ).astype(BF16)
        part[it, j, :, half(which)] = jnp.dot(left, ratio, preferred_element_type=F32)

    def tracks_half(it, j, which):
        b = 2 * j + which
        h_now = hbuf[it + 1, j, :, half(which)]
        h_low = h_now.astype(BF16)
        ratio = ratio_of(b, h_low)
        h_sum = jnp.sum(h_now, axis=1, keepdims=True)
        keep = jnp.zeros((8, 128), F32)
        for tb in range(NT):
            keep = jnp.where(lane == 64 + tb, mask_of(tb, b), keep)
        dacc[...] += h_sum * keep[0:1, :]
        term = lax.dot_general(h_low, ratio, (((1,), (1,)), ((), ())), preferred_element_type=F32)
        for tb in range(NT):
            s = slice(tb * TB, (tb + 1) * TB)
            acc[:, s] += term[:, s] * mask_of(tb, b)

    def spread_w(wt):
        wcol[...] = wt.astype(BF16).astype(F32)
        wrow[...] = wt.T.astype(BF16)

    w_copy_in.wait()
    avail_copy.wait()
    wt0 = wbuf[...]
    spread_w(wt0)
    wth[0, 0] = jnp.concatenate([wt0[:, :HALF], jnp.zeros((K, 64), F32)], axis=1)
    wth[0, 1] = pltpu.roll(wt0[:, 256:640], HALF, 1)

    def w_full(it):
        left = wth[it, 0]
        right = pltpu.roll(wth[it, 1], 64, 1)
        mid = jnp.where(lane64 < 64, left[:, 256:384], right[:, 0:128])
        return jnp.concatenate([left[:, 0:256], mid, right[:, 128:384]], axis=1)

    def start_den(it):
        wt = w_full(it)
        den = jnp.zeros((K, 128), F32)
        for tb in range(NT):
            row = jnp.zeros((8, 128), F32)
            for b in range(NB):
                row = jnp.where(lane == b, mask_of(tb, b), row)
            w_sum = jnp.sum(wt[:, tb * TB : (tb + 1) * TB], axis=1, keepdims=True)
            den = den + w_sum * row[0:1, :]
        dsnd[it] = den
        den_core(it).start()

    def stage_b(it, j):
        core_copy(it, j).wait_recv()
        part[it, j, :, half(c)] = part[it, j, :, half(c)] + crecv[it, j]
        for d in NEAR:
            reduce_copy(it, j, d).start()

        @pl.when(j == 0)
        def _():
            den_core(it).wait_recv()
            dsnd[it + ITERS] = dsnd[it] + dcrecv[it]
            for d in range(1, 8):
                den_copy(it, d).start()

    def stage_c(it, j):
        @pl.when(j == 0)
        def _():
            den_all(it).wait_recv()
            tot = dsnd[it + ITERS, rows_p]
            for d in range(1, 8):
                tot = tot + drecv[it, d - 1]
            dtot[...] = tot

        reduce_all(it, j).wait_recv()
        tot = part[it, j, rows_p, half(c)]
        for d in range(1, 8):
            tot = tot + rrecv[it, j, d - 1]
        den = jnp.sum(jnp.where(lane == 2 * j + c, dtot[...], 0.0), axis=1, keepdims=True)
        hbuf[it + 1, j, rows_p, half(c)] = hbuf[it, j, rows_p, half(c)] * tot / den
        for d in NEAR:
            gather_copy(it, j, d).start()

    def stage_d(it, j):
        gather_all(it, j).wait_recv()
        forward_copy(it, j, c).start()
        tracks_half(it, j, c)

    def stage_e(it, j):
        forward_copy(it, j, 1 - c).wait_recv()
        tracks_half(it, j, 1 - c)

        @pl.when(it == ITERS - 1)
        def _():
            out_copy(j).start()

    def pack_tracks(it):
        full = acc[...]
        dvec = dacc[...]
        gsnd[it, 0, :, 0:256] = full[:, 0:256]
        gsnd[it, 0, :, 256:384] = jnp.where(lane64 < 64, full[:, 256:384], dvec)
        right = pltpu.roll(full[:, 256:640], HALF, 1)
        gsnd[it, 1, :, 0:256] = right[:, 0:256]
        gsnd[it, 1, :, 256:384] = jnp.where(lane64 < 64, right[:, 256:384], dvec)

    def send_tracks(it):
        for k in range(len(SPANS)):
            for d in FAR:
                track_copy(it, k, d).start()

    def wait_tracks(it, k):
        lo, n = SPANS[k]
        ref = grecv.at[it, :, :, lo : lo + n]
        remote(ref, ref, send.at[6], wr.at[it, k], sib).wait_recv()

    def update_w(it):
        divisor = None
        for k, (lo, n) in enumerate(SPANS):
            wait_tracks(it, k)
            tot = gsnd[it, yh, rows_z, lo : lo + n]
            for d in range(1, 16):
                tot = tot + grecv[it, d - 1, :, lo : lo + n]
            if divisor is None:
                divisor = [tot[:, n - 64 + tb : n - 63 + tb] for tb in range(NT)]
            block = (lax.broadcasted_iota(jnp.int32, (8, n), 1) + (yh * HALF + lo)) // TB
            den = jnp.ones((8, n), F32)
            for tb in range(NT):
                den = jnp.where(block == tb, divisor[tb], den)
            wth[it + 1, yh, rows_z, lo : lo + n] = wth[it, yh, rows_z, lo : lo + n] * tot / den
            for d in FAR:
                w_copy(it, k, d).start()

    def wait_w(it):
        remote(grecv.at[it], grecv.at[it], send.at[7], wr.at[it, 3], sib).wait_recv()

    def iteration(it, _):
        acc[...] = jnp.zeros((K, ROWS), F32)
        dacc[...] = jnp.zeros((K, 128), F32)

        def first(j, _):
            @pl.when(it == 0)
            def _():
                h_copy(j).wait()

                @pl.when(j == 0)
                def _():
                    pltpu.make_async_copy(
                        counts.at[:, half(1 - c)], cbuf.at[:, half(1 - c)], csem.at[(1 - c) * NC]
                    ).wait()

                @pl.when(j > 0)
                def _():
                    count_copy(j).wait()

            bins_half(it, j, 1 - c)

            @pl.when((it == 0) & (j == 0))
            def _():
                pl.semaphore_wait(bar, 23)

            core_copy(it, j).start()

            @pl.when(j == 0)
            def _():
                start_den(it)

            @pl.when(j > 0)
            def _():
                stage_b(it, j - 1)

            @pl.when((it == 0) & (j == 0))
            def _():
                pltpu.make_async_copy(counts.at[:, half(c)], cbuf.at[:, half(c)], csem.at[c * NC]).wait()
                lax.fori_loop(1, NC, start_in, 0)

            bins_half(it, j, c)
            return 0

        lax.fori_loop(0, NC, first, 0)
        stage_b(it, NC - 1)

        def second(k, _):
            @pl.when(k < NC)
            def _():
                stage_c(it, k)

            @pl.when((k >= LAG) & (k < NC + LAG))
            def _():
                stage_d(it, k - LAG)

            @pl.when(k > LAG)
            def _():
                stage_e(it, k - LAG - 1)

            return 0

        lax.fori_loop(0, NC + LAG + 1, second, 0)
        pack_tracks(it)
        send_tracks(it)
        update_w(it)
        wait_w(it)
        wt = w_full(it + 1)

        @pl.when(it < ITERS - 1)
        def _():
            spread_w(wt)

        w_out[...] = wt
        return 0

    lax.fori_loop(0, ITERS, iteration, 0)

    def finish(j, _):
        out_copy(j).wait()
        return 0

    lax.fori_loop(0, NC, finish, 0)

    def sent(ref, s):
        remote(ref, ref, send.at[s], dr.at[0, 0], sib).wait_send()

    sent(crecv, 0)
    sent(rrecv, 1)
    sent(rrecv, 2)
    sent(crecv, 3)
    sent(dcrecv, 4)
    sent(drecv, 5)
    sent(grecv, 6)
    sent(grecv, 7)


def settle(w_ref, h_ref, w_out, h_out, sem):
    copies = [pltpu.make_async_copy(w_ref, w_out, sem.at[NC])]
    for j in range(NC):
        span = slice(j * CB, (j + 1) * CB)
        copies.append(pltpu.make_async_copy(h_ref.at[:, span], h_out.at[:, span], sem.at[j]))
    for copy in copies:
        copy.start()
    for copy in copies:
        copy.wait()


def body(counts, avail, track_factors, bin_factors):
    dma = pltpu.SemaphoreType.DMA
    vmem = pltpu.VMEM
    w_new, h_new = pl.pallas_call(
        kernel,
        name="factorize",
        out_shape=(
            pltpu.VMEM((K, ROWS), F32),
            pltpu.VMEM((K, COLS), F32),
        ),
        in_specs=[
            pl.BlockSpec(memory_space=pl.ANY),
            pl.BlockSpec(memory_space=pl.ANY),
            pl.BlockSpec(memory_space=pl.ANY),
            pl.BlockSpec(memory_space=pl.ANY),
        ],
        out_specs=(
            pl.BlockSpec(memory_space=pltpu.VMEM),
            pl.BlockSpec(memory_space=pltpu.VMEM),
        ),
        scratch_shapes=[
            pltpu.SMEM((NT, NB), jnp.int32),
            vmem((K, ROWS), F32),
            vmem((ROWS, COLS), BF16),
            vmem((ITERS + 1, NC, K, CB), F32),
            vmem((ITERS + 1, 2, K, WIDE), F32),
            vmem((ROWS, K), BF16),
            vmem((K, ROWS), F32),
            vmem((ITERS, NC, K, CB), F32),
            vmem((ITERS, NC, K, BB), F32),
            vmem((ITERS, NC, 7, 8, BB), F32),
            vmem((2 * ITERS, K, 128), F32),
            vmem((ITERS, K, 128), F32),
            vmem((ITERS, 7, 8, 128), F32),
            vmem((8, 128), F32),
            vmem((K, ROWS), F32),
            vmem((K, 128), F32),
            vmem((ITERS, 2, K, WIDE), F32),
            vmem((ITERS, 15, 8, WIDE), F32),
            dma((NC + 1,)),
            dma((NC,)),
            dma((NC,)),
            dma((2,)),
            dma((8,)),
            dma((ITERS, NC)),
            dma((ITERS, NC)),
            dma((ITERS, NC)),
            dma((ITERS, NC)),
            dma((ITERS, 2)),
            dma((ITERS, 4)),
        ],
        compiler_params=pltpu.CompilerParams(
            collective_id=0, has_side_effects=True, vmem_limit_bytes=56 * 1024 * 1024
        ),
    )(counts, avail, track_factors.T, bin_factors)
    anywhere = pl.BlockSpec(memory_space=pl.ANY)
    w_new, h_new = pl.pallas_call(
        settle,
        name="settle",
        out_shape=(jax.ShapeDtypeStruct((K, ROWS), F32), jax.ShapeDtypeStruct((K, COLS), F32)),
        in_specs=[anywhere, anywhere],
        out_specs=(anywhere, anywhere),
        scratch_shapes=[dma((NC + 1,))],
    )(*(pltpu.with_memory_space_constraint(v, pltpu.VMEM) for v in (w_new, h_new)))
    return w_new.T, h_new


def solution(mesh):
    placed = (P("track", "genome"), P("track", "genome"), P("track", None), P(None, "genome"))
    return jax.shard_map(
        body,
        mesh=mesh,
        in_specs=placed,
        out_specs=(P("track", None), P(None, "genome")),
        check_vma=False,
    )
```

```python
import jax
import jax.numpy as jnp
from jax import lax
from jax.experimental import pallas as pl
from jax.experimental.pallas import tpu as pltpu
from jax.sharding import PartitionSpec as P

ITERS = 2
K = 64
ROWS = 640
COLS = 6144
TB = 128
BB = 512
NT = ROWS // TB
NB = COLS // BB
NC = NB // 2
HALF = 320
WIDE = 384
LAG = 6
FAR = (12, 11, 13, 4, 10, 14, 3, 5, 9, 15, 2, 6, 8, 1, 7)
NEAR = (6, 2, 5, 1, 7, 3, 4)
PIECES = 1
SPANS = ((256, 128), (0, 256))
CB = 2 * BB
MESH = pl.DeviceIdType.MESH
F32 = jnp.float32
BF16 = jnp.bfloat16


def kernel(
    counts, avail_in, w_in, h_in, w_out, h_out,
    avail, wbuf, cbuf, hbuf, wth, wrow, wcol, part, crecv, rrecv, dsnd, dcrecv, drecv, dtot,
    acc, dacc, gsnd, grecv,
    csem, hsem, osem, wsem, send, cr, rr, gr, fr, dr, wr,
):
    g = lax.axis_index("genome")
    t = lax.axis_index("track")
    yh, z = g // 8, g % 8
    p, c = t // 2, t % 2
    y, x = p // 4, p % 4
    sib = (g, p * 2 + (1 - c))

    def tpeer(d):
        q = ((y + d // 4) % 2) * 4 + (x + d % 4) % 4
        return q, (g, q * 2 + c)

    def gpeer(d):
        qh, qz = (yh + d // 8) % 2, (z + d % 8) % 8
        return qh, qz, (qh * 8 + qz, t)

    def cols(j):
        return pl.ds(pl.multiple_of(j * CB, CB), CB)

    def half(which):
        return pl.ds(pl.multiple_of(which * BB, BB), BB)

    def count_copy(j):
        return pltpu.make_async_copy(counts.at[:, cols(j)], cbuf.at[:, cols(j)], csem.at[j])

    def h_copy(j):
        return pltpu.make_async_copy(h_in.at[:, cols(j)], hbuf.at[0, j], hsem.at[j])

    def out_copy(j):
        return pltpu.make_async_copy(hbuf.at[ITERS, j], h_out.at[:, cols(j)], osem.at[0])

    def start_in(j, _):
        h_copy(j).start()
        count_copy(j).start()
        return 0

    def first_in(which):
        rows = ROWS // PIECES
        return [
            pltpu.make_async_copy(
                counts.at[r * rows : (r + 1) * rows, half(which)],
                cbuf.at[r * rows : (r + 1) * rows, half(which)],
                csem.at[which * NC],
            )
            for r in range(PIECES)
        ]

    w_copy_in = pltpu.make_async_copy(w_in, wbuf, wsem.at[0])
    w_copy_in.start()
    avail_copy = pltpu.make_async_copy(avail_in, avail, wsem.at[1])
    avail_copy.start()
    h_copy(0).start()
    for copy in first_in(1 - c) + first_in(c):
        copy.start()

    bar = pltpu.get_barrier_semaphore()
    for d in FAR:
        pl.semaphore_signal(bar, inc=1, device_id=gpeer(d)[2], device_id_type=MESH)
    for d in range(1, 8):
        pl.semaphore_signal(bar, inc=1, device_id=tpeer(d)[1], device_id_type=MESH)
    pl.semaphore_signal(bar, inc=1, device_id=sib, device_id_type=MESH)

    def remote(src, dst, s, r, dev):
        return pltpu.make_async_remote_copy(
            src_ref=src, dst_ref=dst, send_sem=s, recv_sem=r, device_id=dev, device_id_type=MESH
        )

    rows_p = pl.ds(pl.multiple_of(p * 8, 8), 8)
    rows_z = pl.ds(pl.multiple_of(z * 8, 8), 8)

    def core_copy(it, j):
        return remote(part.at[it, j, :, half(1 - c)], crecv.at[it, j], send.at[0], cr.at[j], sib)

    def reduce_copy(it, j, d):
        q, dev = tpeer(d)
        rows = pl.ds(pl.multiple_of(q * 8, 8), 8)
        return remote(part.at[it, j, rows, half(c)], rrecv.at[it, j, d - 1], send.at[1], rr.at[j], dev)

    def reduce_all(it, j):
        return remote(rrecv.at[it, j], rrecv.at[it, j], send.at[1], rr.at[j], sib)

    def gather_copy(it, j, d):
        ref = hbuf.at[it + 1, j, rows_p, half(c)]
        return remote(ref, ref, send.at[2], gr.at[j], tpeer(d)[1])

    def gather_all(it, j):
        return remote(rrecv.at[it, j], rrecv.at[it, j], send.at[2], gr.at[j], sib)

    def forward_copy(it, j, which):
        ref = hbuf.at[it + 1, j, :, half(which)]
        return remote(ref, ref, send.at[3], fr.at[j], sib)

    def den_core(it):
        return remote(dsnd.at[it], dcrecv.at[it], send.at[4], dr.at[it, 0], sib)

    def den_copy(it, d):
        q, dev = tpeer(d)
        rows = pl.ds(pl.multiple_of(q * 8, 8), 8)
        return remote(dsnd.at[it + ITERS, rows], drecv.at[it, d - 1], send.at[5], dr.at[it, 1], dev)

    def den_all(it):
        return remote(drecv.at[it], drecv.at[it], send.at[5], dr.at[it, 1], sib)

    def track_copy(it, k, d):
        qh, qz, dev = gpeer(d)
        rows = pl.ds(pl.multiple_of(qz * 8, 8), 8)
        lo, n = SPANS[k]
        return remote(
            gsnd.at[it, qh, rows, lo : lo + n], grecv.at[it, d - 1, :, lo : lo + n], send.at[6], wr.at[it, k], dev
        )

    def w_copy(it, k, d):
        lo, n = SPANS[k]
        ref = wth.at[it + 1, yh, rows_z, lo : lo + n]
        return remote(ref, ref, send.at[7], wr.at[it, 3], gpeer(d)[2])

    lane = lax.broadcasted_iota(jnp.int32, (8, 128), 1)
    lane64 = lax.broadcasted_iota(jnp.int32, (K, 128), 1)

    def mask_of(tb, b):
        return avail[tb, b].astype(F32)

    def ratio_of(b, h_low):
        recon = jnp.dot(wrow[...], h_low, preferred_element_type=F32)
        return (cbuf[:, half(b)].astype(F32) / recon).astype(BF16)

    def bins_half(it, j, which):
        b = 2 * j + which
        ratio = ratio_of(b, hbuf[it, j, :, half(which)].astype(BF16))
        left = jnp.concatenate(
            [wcol[:, tb * TB : (tb + 1) * TB] * mask_of(tb, b) for tb in range(NT)], axis=1
        ).astype(BF16)
        part[it, j, :, half(which)] = jnp.dot(left, ratio, preferred_element_type=F32)

    def tracks_half(it, j, which):
        b = 2 * j + which
        h_now = hbuf[it + 1, j, :, half(which)]
        h_low = h_now.astype(BF16)
        ratio = ratio_of(b, h_low)
        h_sum = jnp.sum(h_now, axis=1, keepdims=True)
        keep = jnp.zeros((8, 128), F32)
        for tb in range(NT):
            keep = jnp.where(lane == 64 + tb, mask_of(tb, b), keep)
        dacc[...] += h_sum * keep[0:1, :]
        term = lax.dot_general(h_low, ratio, (((1,), (1,)), ((), ())), preferred_element_type=F32)
        for tb in range(NT):
            s = slice(tb * TB, (tb + 1) * TB)
            acc[:, s] += term[:, s] * mask_of(tb, b)

    def spread_w(wt):
        wcol[...] = wt.astype(BF16).astype(F32)
        wrow[...] = wt.T.astype(BF16)

    w_copy_in.wait()
    avail_copy.wait()
    wt0 = wbuf[...]
    spread_w(wt0)
    wth[0, 0] = jnp.concatenate([wt0[:, :HALF], jnp.zeros((K, 64), F32)], axis=1)
    wth[0, 1] = pltpu.roll(wt0[:, 256:640], HALF, 1)

    def w_full(it):
        left = wth[it, 0]
        right = pltpu.roll(wth[it, 1], 64, 1)
        mid = jnp.where(lane64 < 64, left[:, 256:384], right[:, 0:128])
        return jnp.concatenate([left[:, 0:256], mid, right[:, 128:384]], axis=1)

    def start_den(it):
        wt = w_full(it)
        den = jnp.zeros((K, 128), F32)
        for tb in range(NT):
            row = jnp.zeros((8, 128), F32)
            for b in range(NB):
                row = jnp.where(lane == b, mask_of(tb, b), row)
            w_sum = jnp.sum(wt[:, tb * TB : (tb + 1) * TB], axis=1, keepdims=True)
            den = den + w_sum * row[0:1, :]
        dsnd[it] = den
        den_core(it).start()

    def stage_b(it, j):
        core_copy(it, j).wait_recv()
        part[it, j, :, half(c)] = part[it, j, :, half(c)] + crecv[it, j]
        for d in NEAR:
            reduce_copy(it, j, d).start()

        @pl.when(j == 0)
        def _():
            den_core(it).wait_recv()
            dsnd[it + ITERS] = dsnd[it] + dcrecv[it]
            for d in range(1, 8):
                den_copy(it, d).start()

    def stage_c(it, j):
        @pl.when(j == 0)
        def _():
            den_all(it).wait_recv()
            tot = dsnd[it + ITERS, rows_p]
            for d in range(1, 8):
                tot = tot + drecv[it, d - 1]
            dtot[...] = tot

        reduce_all(it, j).wait_recv()
        tot = part[it, j, rows_p, half(c)]
        for d in range(1, 8):
            tot = tot + rrecv[it, j, d - 1]
        den = jnp.sum(jnp.where(lane == 2 * j + c, dtot[...], 0.0), axis=1, keepdims=True)
        hbuf[it + 1, j, rows_p, half(c)] = hbuf[it, j, rows_p, half(c)] * tot / den
        for d in NEAR:
            gather_copy(it, j, d).start()

    def stage_d(it, j):
        gather_all(it, j).wait_recv()
        forward_copy(it, j, c).start()
        tracks_half(it, j, c)

    def stage_e(it, j):
        forward_copy(it, j, 1 - c).wait_recv()
        tracks_half(it, j, 1 - c)

        @pl.when(it == ITERS - 1)
        def _():
            out_copy(j).start()

    def pack_tracks(it):
        full = acc[...]
        dvec = dacc[...]
        gsnd[it, 0, :, 0:256] = full[:, 0:256]
        gsnd[it, 0, :, 256:384] = jnp.where(lane64 < 64, full[:, 256:384], dvec)
        right = pltpu.roll(full[:, 256:640], HALF, 1)
        gsnd[it, 1, :, 0:256] = right[:, 0:256]
        gsnd[it, 1, :, 256:384] = jnp.where(lane64 < 64, right[:, 256:384], dvec)

    def send_tracks(it):
        for k in range(len(SPANS)):
            for d in FAR:
                track_copy(it, k, d).start()

    def wait_tracks(it, k):
        lo, n = SPANS[k]
        ref = grecv.at[it, :, :, lo : lo + n]
        remote(ref, ref, send.at[6], wr.at[it, k], sib).wait_recv()

    def update_w(it):
        divisor = None
        for k, (lo, n) in enumerate(SPANS):
            wait_tracks(it, k)
            tot = gsnd[it, yh, rows_z, lo : lo + n]
            for d in range(1, 16):
                tot = tot + grecv[it, d - 1, :, lo : lo + n]
            if divisor is None:
                divisor = [tot[:, n - 64 + tb : n - 63 + tb] for tb in range(NT)]
            block = (lax.broadcasted_iota(jnp.int32, (8, n), 1) + (yh * HALF + lo)) // TB
            den = jnp.ones((8, n), F32)
            for tb in range(NT):
                den = jnp.where(block == tb, divisor[tb], den)
            wth[it + 1, yh, rows_z, lo : lo + n] = wth[it, yh, rows_z, lo : lo + n] * tot / den
            for d in FAR:
                w_copy(it, k, d).start()

    def wait_w(it):
        remote(grecv.at[it], grecv.at[it], send.at[7], wr.at[it, 3], sib).wait_recv()

    def iteration(it, _):
        acc[...] = jnp.zeros((K, ROWS), F32)
        dacc[...] = jnp.zeros((K, 128), F32)

        def first(j, _):
            @pl.when(it == 0)
            def _():
                h_copy(j).wait()

                @pl.when(j == 0)
                def _():
                    pltpu.make_async_copy(
                        counts.at[:, half(1 - c)], cbuf.at[:, half(1 - c)], csem.at[(1 - c) * NC]
                    ).wait()
                    lax.fori_loop(1, NC, start_in, 0)

                @pl.when(j > 0)
                def _():
                    count_copy(j).wait()

            bins_half(it, j, 1 - c)

            @pl.when((it == 0) & (j == 0))
            def _():
                pl.semaphore_wait(bar, 23)

            core_copy(it, j).start()

            @pl.when(j == 0)
            def _():
                start_den(it)

            @pl.when(j > 0)
            def _():
                stage_b(it, j - 1)

            @pl.when((it == 0) & (j == 0))
            def _():
                pltpu.make_async_copy(counts.at[:, half(c)], cbuf.at[:, half(c)], csem.at[c * NC]).wait()

            bins_half(it, j, c)
            return 0

        lax.fori_loop(0, NC, first, 0)
        stage_b(it, NC - 1)

        def second(k, _):
            @pl.when(k < NC)
            def _():
                stage_c(it, k)

            @pl.when((k >= LAG) & (k < NC + LAG))
            def _():
                stage_d(it, k - LAG)

            @pl.when(k > LAG)
            def _():
                stage_e(it, k - LAG - 1)

            return 0

        lax.fori_loop(0, NC + LAG + 1, second, 0)
        pack_tracks(it)
        send_tracks(it)
        update_w(it)
        wait_w(it)
        wt = w_full(it + 1)

        @pl.when(it < ITERS - 1)
        def _():
            spread_w(wt)

        w_out[...] = wt
        return 0

    lax.fori_loop(0, ITERS, iteration, 0)

    pltpu.make_async_copy(hbuf.at[ITERS], hbuf.at[ITERS], osem.at[0]).wait()

    def sent(ref, s):
        remote(ref, ref, send.at[s], dr.at[0, 0], sib).wait_send()

    sent(crecv, 0)
    sent(rrecv, 1)
    sent(rrecv, 2)
    sent(crecv, 3)
    sent(dcrecv, 4)
    sent(drecv, 5)
    sent(grecv, 6)
    sent(grecv, 7)


def settle(w_ref, h_ref, w_out, h_out, sem):
    copies = [pltpu.make_async_copy(w_ref, w_out, sem.at[NC])]
    for j in range(NC):
        span = slice(j * CB, (j + 1) * CB)
        copies.append(pltpu.make_async_copy(h_ref.at[:, span], h_out.at[:, span], sem.at[j]))
    for copy in copies:
        copy.start()
    for copy in copies:
        copy.wait()


def body(counts, avail, track_factors, bin_factors):
    dma = pltpu.SemaphoreType.DMA
    vmem = pltpu.VMEM
    w_new, h_new = pl.pallas_call(
        kernel,
        name="factorize",
        out_shape=(
            pltpu.VMEM((K, ROWS), F32),
            pltpu.VMEM((K, COLS), F32),
        ),
        in_specs=[
            pl.BlockSpec(memory_space=pl.ANY),
            pl.BlockSpec(memory_space=pl.ANY),
            pl.BlockSpec(memory_space=pl.ANY),
            pl.BlockSpec(memory_space=pl.ANY),
        ],
        out_specs=(
            pl.BlockSpec(memory_space=pltpu.VMEM),
            pl.BlockSpec(memory_space=pltpu.VMEM),
        ),
        scratch_shapes=[
            pltpu.SMEM((NT, NB), jnp.int32),
            vmem((K, ROWS), F32),
            vmem((ROWS, COLS), BF16),
            vmem((ITERS + 1, NC, K, CB), F32),
            vmem((ITERS + 1, 2, K, WIDE), F32),
            vmem((ROWS, K), BF16),
            vmem((K, ROWS), F32),
            vmem((ITERS, NC, K, CB), F32),
            vmem((ITERS, NC, K, BB), F32),
            vmem((ITERS, NC, 7, 8, BB), F32),
            vmem((2 * ITERS, K, 128), F32),
            vmem((ITERS, K, 128), F32),
            vmem((ITERS, 7, 8, 128), F32),
            vmem((8, 128), F32),
            vmem((K, ROWS), F32),
            vmem((K, 128), F32),
            vmem((ITERS, 2, K, WIDE), F32),
            vmem((ITERS, 15, 8, WIDE), F32),
            dma((NC + 1,)),
            dma((NC,)),
            dma((1,)),
            dma((2,)),
            dma((8,)),
            dma((NC,)),
            dma((NC,)),
            dma((NC,)),
            dma((NC,)),
            dma((ITERS, 2)),
            dma((ITERS, 4)),
        ],
        compiler_params=pltpu.CompilerParams(
            collective_id=0, has_side_effects=True, vmem_limit_bytes=56 * 1024 * 1024
        ),
    )(counts, avail, track_factors.T, bin_factors)
    anywhere = pl.BlockSpec(memory_space=pl.ANY)
    w_new, h_new = pl.pallas_call(
        settle,
        name="settle",
        out_shape=(jax.ShapeDtypeStruct((K, ROWS), F32), jax.ShapeDtypeStruct((K, COLS), F32)),
        in_specs=[anywhere, anywhere],
        out_specs=(anywhere, anywhere),
        scratch_shapes=[dma((NC + 1,))],
    )(*(pltpu.with_memory_space_constraint(v, pltpu.VMEM) for v in (w_new, h_new)))
    return w_new.T, h_new


def solution(mesh):
    placed = (P("track", "genome"), P("track", "genome"), P("track", None), P(None, "genome"))
    return jax.shard_map(
        body,
        mesh=mesh,
        in_specs=placed,
        out_specs=(P("track", None), P(None, "genome")),
        check_vma=False,
    )
```

```python
import jax
import jax.numpy as jnp
from jax import lax
from jax.experimental import pallas as pl
from jax.experimental.pallas import tpu as pltpu
from jax.sharding import PartitionSpec as P

ITERS = 2
K = 64
ROWS = 640
COLS = 6144
TB = 128
BB = 512
NT = ROWS // TB
NB = COLS // BB
NC = NB // 2
HALF = 320
WIDE = 384
LAG = 6
FAR = (12, 11, 13, 4, 10, 14, 3, 5, 9, 15, 2, 6, 8, 1, 7)
NEAR = (6, 2, 5, 1, 7, 3, 4)
PIECES = 1
SPANS = ((256, 128), (0, 256))
CB = 2 * BB
MESH = pl.DeviceIdType.MESH
F32 = jnp.float32
BF16 = jnp.bfloat16


def kernel(
    counts, avail_in, w_in, h_in, w_out, h_out,
    avail, wbuf, cbuf, hbuf, wth, wrow, wcol, part, crecv, rrecv, dsnd, dcrecv, drecv, dtot,
    acc, dacc, gsnd, grecv,
    csem, hsem, osem, wsem, send, cr, rr, gr, fr, dr, wr,
):
    g = lax.axis_index("genome")
    t = lax.axis_index("track")
    yh, z = g // 8, g % 8
    p, c = t // 2, t % 2
    y, x = p // 4, p % 4
    sib = (g, p * 2 + (1 - c))

    def tpeer(d):
        q = ((y + d // 4) % 2) * 4 + (x + d % 4) % 4
        return q, (g, q * 2 + c)

    def gpeer(d):
        qh, qz = (yh + d // 8) % 2, (z + d % 8) % 8
        return qh, qz, (qh * 8 + qz, t)

    def cols(j):
        return pl.ds(pl.multiple_of(j * CB, CB), CB)

    def half(which):
        return pl.ds(pl.multiple_of(which * BB, BB), BB)

    def count_copy(j):
        return pltpu.make_async_copy(counts.at[:, cols(j)], cbuf.at[:, cols(j)], csem.at[j])

    def h_copy(j):
        return pltpu.make_async_copy(h_in.at[:, cols(j)], hbuf.at[0, j], hsem.at[j])

    def out_copy(j):
        return pltpu.make_async_copy(hbuf.at[ITERS, j], h_out.at[:, cols(j)], osem.at[0])

    def start_in(j, _):
        h_copy(j).start()
        count_copy(j).start()
        return 0

    def first_in(which):
        rows = ROWS // PIECES
        return [
            pltpu.make_async_copy(
                counts.at[r * rows : (r + 1) * rows, half(which)],
                cbuf.at[r * rows : (r + 1) * rows, half(which)],
                csem.at[which * NC],
            )
            for r in range(PIECES)
        ]

    w_copy_in = pltpu.make_async_copy(w_in, wbuf, wsem.at[0])
    w_copy_in.start()
    avail_copy = pltpu.make_async_copy(avail_in, avail, wsem.at[1])
    avail_copy.start()
    h_copy(0).start()
    for copy in first_in(1 - c) + first_in(c):
        copy.start()

    bar = pltpu.get_barrier_semaphore()
    for d in FAR:
        pl.semaphore_signal(bar, inc=1, device_id=gpeer(d)[2], device_id_type=MESH)
    for d in range(1, 8):
        pl.semaphore_signal(bar, inc=1, device_id=tpeer(d)[1], device_id_type=MESH)
    pl.semaphore_signal(bar, inc=1, device_id=sib, device_id_type=MESH)

    def remote(src, dst, s, r, dev):
        return pltpu.make_async_remote_copy(
            src_ref=src, dst_ref=dst, send_sem=s, recv_sem=r, device_id=dev, device_id_type=MESH
        )

    rows_p = pl.ds(pl.multiple_of(p * 8, 8), 8)
    rows_z = pl.ds(pl.multiple_of(z * 8, 8), 8)

    def core_copy(it, j):
        return remote(part.at[it, j, :, half(1 - c)], crecv.at[it, j], send.at[0], cr.at[j], sib)

    def reduce_copy(it, j, d):
        q, dev = tpeer(d)
        rows = pl.ds(pl.multiple_of(q * 8, 8), 8)
        return remote(part.at[it, j, rows, half(c)], rrecv.at[it, j, d - 1], send.at[1], rr.at[j], dev)

    def reduce_all(it, j):
        return remote(rrecv.at[it, j], rrecv.at[it, j], send.at[1], rr.at[j], sib)

    def gather_copy(it, j, d):
        ref = hbuf.at[it + 1, j, rows_p, half(c)]
        return remote(ref, ref, send.at[2], gr.at[j], tpeer(d)[1])

    def gather_all(it, j):
        return remote(rrecv.at[it, j], rrecv.at[it, j], send.at[2], gr.at[j], sib)

    def forward_copy(it, j, which):
        ref = hbuf.at[it + 1, j, :, half(which)]
        return remote(ref, ref, send.at[3], fr.at[j], sib)

    def den_core(it):
        return remote(dsnd.at[it], dcrecv.at[it], send.at[4], dr.at[0], sib)

    def den_copy(it, d):
        q, dev = tpeer(d)
        rows = pl.ds(pl.multiple_of(q * 8, 8), 8)
        return remote(dsnd.at[it + ITERS, rows], drecv.at[it, d - 1], send.at[5], dr.at[1], dev)

    def den_all(it):
        return remote(drecv.at[it], drecv.at[it], send.at[5], dr.at[1], sib)

    def track_copy(it, k, d):
        qh, qz, dev = gpeer(d)
        rows = pl.ds(pl.multiple_of(qz * 8, 8), 8)
        lo, n = SPANS[k]
        return remote(
            gsnd.at[it, qh, rows, lo : lo + n], grecv.at[it, d - 1, :, lo : lo + n], send.at[6], wr.at[k], dev
        )

    def w_copy(it, k, d):
        lo, n = SPANS[k]
        ref = wth.at[it + 1, yh, rows_z, lo : lo + n]
        return remote(ref, ref, send.at[7], wr.at[2], gpeer(d)[2])

    lane = lax.broadcasted_iota(jnp.int32, (8, 128), 1)
    lane64 = lax.broadcasted_iota(jnp.int32, (K, 128), 1)

    def mask_of(tb, b):
        return avail[tb, b].astype(F32)

    def ratio_of(b, h_low):
        recon = jnp.dot(wrow[...], h_low, preferred_element_type=F32)
        return (cbuf[:, half(b)].astype(F32) / recon).astype(BF16)

    def bins_half(it, j, which):
        b = 2 * j + which
        ratio = ratio_of(b, hbuf[it, j, :, half(which)].astype(BF16))
        left = jnp.concatenate(
            [wcol[:, tb * TB : (tb + 1) * TB] * mask_of(tb, b) for tb in range(NT)], axis=1
        ).astype(BF16)
        part[it, j, :, half(which)] = jnp.dot(left, ratio, preferred_element_type=F32)

    def tracks_half(it, j, which):
        b = 2 * j + which
        h_now = hbuf[it + 1, j, :, half(which)]
        h_low = h_now.astype(BF16)
        ratio = ratio_of(b, h_low)
        h_sum = jnp.sum(h_now, axis=1, keepdims=True)
        keep = jnp.zeros((8, 128), F32)
        for tb in range(NT):
            keep = jnp.where(lane == 64 + tb, mask_of(tb, b), keep)
        dacc[...] += h_sum * keep[0:1, :]
        term = lax.dot_general(h_low, ratio, (((1,), (1,)), ((), ())), preferred_element_type=F32)
        for tb in range(NT):
            s = slice(tb * TB, (tb + 1) * TB)
            acc[:, s] += term[:, s] * mask_of(tb, b)

    def spread_w(wt):
        wcol[...] = wt.astype(BF16).astype(F32)
        wrow[...] = wt.T.astype(BF16)

    w_copy_in.wait()
    avail_copy.wait()
    wt0 = wbuf[...]
    spread_w(wt0)
    wth[0, 0] = jnp.concatenate([wt0[:, :HALF], jnp.zeros((K, 64), F32)], axis=1)
    wth[0, 1] = pltpu.roll(wt0[:, 256:640], HALF, 1)

    def w_full(it):
        left = wth[it, 0]
        right = pltpu.roll(wth[it, 1], 64, 1)
        mid = jnp.where(lane64 < 64, left[:, 256:384], right[:, 0:128])
        return jnp.concatenate([left[:, 0:256], mid, right[:, 128:384]], axis=1)

    def start_den(it):
        wt = w_full(it)
        den = jnp.zeros((K, 128), F32)
        for tb in range(NT):
            row = jnp.zeros((8, 128), F32)
            for b in range(NB):
                row = jnp.where(lane == b, mask_of(tb, b), row)
            w_sum = jnp.sum(wt[:, tb * TB : (tb + 1) * TB], axis=1, keepdims=True)
            den = den + w_sum * row[0:1, :]
        dsnd[it] = den
        den_core(it).start()

    def stage_b(it, j):
        core_copy(it, j).wait_recv()
        part[it, j, :, half(c)] = part[it, j, :, half(c)] + crecv[it, j]
        for d in NEAR:
            reduce_copy(it, j, d).start()

        @pl.when(j == 0)
        def _():
            den_core(it).wait_recv()
            dsnd[it + ITERS] = dsnd[it] + dcrecv[it]
            for d in range(1, 8):
                den_copy(it, d).start()

    def stage_c(it, j):
        @pl.when(j == 0)
        def _():
            den_all(it).wait_recv()
            tot = dsnd[it + ITERS, rows_p]
            for d in range(1, 8):
                tot = tot + drecv[it, d - 1]
            dtot[...] = tot

        reduce_all(it, j).wait_recv()
        tot = part[it, j, rows_p, half(c)]
        for d in range(1, 8):
            tot = tot + rrecv[it, j, d - 1]
        den = jnp.sum(jnp.where(lane == 2 * j + c, dtot[...], 0.0), axis=1, keepdims=True)
        hbuf[it + 1, j, rows_p, half(c)] = hbuf[it, j, rows_p, half(c)] * tot / den
        for d in NEAR:
            gather_copy(it, j, d).start()

    def stage_d(it, j):
        gather_all(it, j).wait_recv()
        forward_copy(it, j, c).start()
        tracks_half(it, j, c)

    def stage_e(it, j):
        forward_copy(it, j, 1 - c).wait_recv()
        tracks_half(it, j, 1 - c)

        @pl.when(it == ITERS - 1)
        def _():
            out_copy(j).start()

    def pack_tracks(it):
        full = acc[...]
        dvec = dacc[...]
        gsnd[it, 0, :, 0:256] = full[:, 0:256]
        gsnd[it, 0, :, 256:384] = jnp.where(lane64 < 64, full[:, 256:384], dvec)
        right = pltpu.roll(full[:, 256:640], HALF, 1)
        gsnd[it, 1, :, 0:256] = right[:, 0:256]
        gsnd[it, 1, :, 256:384] = jnp.where(lane64 < 64, right[:, 256:384], dvec)

    def send_tracks(it):
        for k in range(len(SPANS)):
            for d in FAR:
                track_copy(it, k, d).start()

    def wait_tracks(it, k):
        lo, n = SPANS[k]
        ref = grecv.at[it, :, :, lo : lo + n]
        remote(ref, ref, send.at[6], wr.at[k], sib).wait_recv()

    def update_w(it):
        divisor = None
        for k, (lo, n) in enumerate(SPANS):
            wait_tracks(it, k)
            tot = gsnd[it, yh, rows_z, lo : lo + n]
            for d in range(1, 16):
                tot = tot + grecv[it, d - 1, :, lo : lo + n]
            if divisor is None:
                divisor = [tot[:, n - 64 + tb : n - 63 + tb] for tb in range(NT)]
            block = (lax.broadcasted_iota(jnp.int32, (8, n), 1) + (yh * HALF + lo)) // TB
            den = jnp.ones((8, n), F32)
            for tb in range(NT):
                den = jnp.where(block == tb, divisor[tb], den)
            wth[it + 1, yh, rows_z, lo : lo + n] = wth[it, yh, rows_z, lo : lo + n] * tot / den
            for d in FAR:
                w_copy(it, k, d).start()

    def wait_w(it):
        remote(grecv.at[it], grecv.at[it], send.at[7], wr.at[2], sib).wait_recv()

    def iteration(it, _):
        acc[...] = jnp.zeros((K, ROWS), F32)
        dacc[...] = jnp.zeros((K, 128), F32)

        def first(j, _):
            @pl.when(it == 0)
            def _():
                h_copy(j).wait()

                @pl.when(j == 0)
                def _():
                    pltpu.make_async_copy(
                        counts.at[:, half(1 - c)], cbuf.at[:, half(1 - c)], csem.at[(1 - c) * NC]
                    ).wait()
                    lax.fori_loop(1, NC, start_in, 0)

                @pl.when(j > 0)
                def _():
                    count_copy(j).wait()

            bins_half(it, j, 1 - c)

            @pl.when((it == 0) & (j == 0))
            def _():
                pl.semaphore_wait(bar, 23)

            core_copy(it, j).start()

            @pl.when(j == 0)
            def _():
                start_den(it)

            @pl.when(j > 0)
            def _():
                stage_b(it, j - 1)

            @pl.when((it == 0) & (j == 0))
            def _():
                pltpu.make_async_copy(counts.at[:, half(c)], cbuf.at[:, half(c)], csem.at[c * NC]).wait()

            bins_half(it, j, c)
            return 0

        lax.fori_loop(0, NC, first, 0)
        stage_c(it, 0)
        stage_b(it, NC - 1)

        def second(k, _):
            @pl.when((k > 0) & (k < NC))
            def _():
                stage_c(it, k)

            @pl.when((k >= LAG) & (k < NC + LAG))
            def _():
                stage_d(it, k - LAG)

            @pl.when(k > LAG)
            def _():
                stage_e(it, k - LAG - 1)

            return 0

        lax.fori_loop(0, NC + LAG + 1, second, 0)
        pack_tracks(it)
        send_tracks(it)
        update_w(it)
        wait_w(it)
        wt = w_full(it + 1)

        @pl.when(it < ITERS - 1)
        def _():
            spread_w(wt)

        w_out[...] = wt
        return 0

    lax.fori_loop(0, ITERS, iteration, 0)

    pltpu.make_async_copy(hbuf.at[ITERS], hbuf.at[ITERS], osem.at[0]).wait()

    def sent(ref, s):
        remote(ref, ref, send.at[s], dr.at[0], sib).wait_send()

    sent(crecv, 0)
    sent(rrecv, 1)
    sent(rrecv, 2)
    sent(crecv, 3)
    sent(dcrecv, 4)
    sent(drecv, 5)
    sent(grecv, 6)
    sent(grecv, 7)


def settle(w_ref, h_ref, w_out, h_out, sem):
    copies = [pltpu.make_async_copy(w_ref, w_out, sem.at[NC])]
    for j in range(NC):
        span = slice(j * CB, (j + 1) * CB)
        copies.append(pltpu.make_async_copy(h_ref.at[:, span], h_out.at[:, span], sem.at[j]))
    for copy in copies:
        copy.start()
    for copy in copies:
        copy.wait()


def body(counts, avail, track_factors, bin_factors):
    dma = pltpu.SemaphoreType.DMA
    vmem = pltpu.VMEM
    w_new, h_new = pl.pallas_call(
        kernel,
        name="factorize",
        out_shape=(
            pltpu.VMEM((K, ROWS), F32),
            pltpu.VMEM((K, COLS), F32),
        ),
        in_specs=[
            pl.BlockSpec(memory_space=pl.ANY),
            pl.BlockSpec(memory_space=pl.ANY),
            pl.BlockSpec(memory_space=pl.ANY),
            pl.BlockSpec(memory_space=pl.ANY),
        ],
        out_specs=(
            pl.BlockSpec(memory_space=pltpu.VMEM),
            pl.BlockSpec(memory_space=pltpu.VMEM),
        ),
        scratch_shapes=[
            pltpu.SMEM((NT, NB), jnp.int32),
            vmem((K, ROWS), F32),
            vmem((ROWS, COLS), BF16),
            vmem((ITERS + 1, NC, K, CB), F32),
            vmem((ITERS + 1, 2, K, WIDE), F32),
            vmem((ROWS, K), BF16),
            vmem((K, ROWS), F32),
            vmem((ITERS, NC, K, CB), F32),
            vmem((ITERS, NC, K, BB), F32),
            vmem((ITERS, NC, 7, 8, BB), F32),
            vmem((2 * ITERS, K, 128), F32),
            vmem((ITERS, K, 128), F32),
            vmem((ITERS, 7, 8, 128), F32),
            vmem((8, 128), F32),
            vmem((K, ROWS), F32),
            vmem((K, 128), F32),
            vmem((ITERS, 2, K, WIDE), F32),
            vmem((ITERS, 15, 8, WIDE), F32),
            dma((NC + 1,)),
            dma((NC,)),
            dma((1,)),
            dma((2,)),
            dma((8,)),
            dma((NC,)),
            dma((NC,)),
            dma((NC,)),
            dma((NC,)),
            dma((2,)),
            dma((3,)),
        ],
        compiler_params=pltpu.CompilerParams(
            collective_id=0, has_side_effects=True, vmem_limit_bytes=56 * 1024 * 1024
        ),
    )(counts, avail, track_factors.T, bin_factors)
    anywhere = pl.BlockSpec(memory_space=pl.ANY)
    w_new, h_new = pl.pallas_call(
        settle,
        name="settle",
        out_shape=(jax.ShapeDtypeStruct((K, ROWS), F32), jax.ShapeDtypeStruct((K, COLS), F32)),
        in_specs=[anywhere, anywhere],
        out_specs=(anywhere, anywhere),
        scratch_shapes=[dma((NC + 1,))],
    )(*(pltpu.with_memory_space_constraint(v, pltpu.VMEM) for v in (w_new, h_new)))
    return w_new.T, h_new


def solution(mesh):
    placed = (P("track", "genome"), P("track", "genome"), P("track", None), P(None, "genome"))
    return jax.shard_map(
        body,
        mesh=mesh,
        in_specs=placed,
        out_specs=(P("track", None), P(None, "genome")),
        check_vma=False,
    )
```
